512 devices in a mesh: seq: 16 (over y, z_lo), res: 32 (over x, z_hi, core).
Axes of the slice: x: 4, y: 8, z: 8 (z_hi: 4, z_lo: 2; z = z_hi * 2 + z_lo), core: 2. Of those that a mesh axis runs over, the one named last changes fastest.
Arguments:
- alignment_embedding: bfloat16 [256, 1024, 256], P('seq', 'res'), may hold values from -6 to 6
- heed_layer_gain: float32 [256], replicated, may hold values from 0.25 to 1.75
- heed_layer_shift: float32 [256], replicated, may hold values from -1.75 to 1.75
- probe_weights: bfloat16 [256, 256], replicated, may hold values from -48 to 48
- lookup_weights: bfloat16 [256, 256], replicated, may hold values from -1 to 1
- content_weights: bfloat16 [256, 256], replicated, may hold values from -0.375 to 0.375
- sigmoid_weights: bfloat16 [256, 256], replicated, may hold values from -0.375 to 0.375
- sigmoid_shift: float32 [256], replicated, may hold values from -6 to 6
- final_weights: bfloat16 [256, 256], replicated, may hold values from -1.5 to 1.5
- final_shift: float32 [256], replicated, may hold values from -1.75 to 1.75
- tensor_layer_gain: float32 [256], replicated, may hold values from 0.25 to 1.75
- tensor_layer_shift: float32 [256], replicated, may hold values from -1.75 to 1.75
- first_factor_weights: bfloat16 [256, 32], replicated, may hold values from -0.375 to 0.375
- second_factor_weights: bfloat16 [256, 32], replicated, may hold values from -0.375 to 0.375
- couple_weights: bfloat16 [1024, 128], replicated, may hold values from -3 to 3
- couple_shift: float32 [128], replicated, may hold values from -1.75 to 1.75
Outputs:
- updated: bfloat16 [256, 1024, 256], P('seq', 'res')
- pair_update: bfloat16 [1024, 1024, 128], P('seq', 'res')
The draws below stay inside these ranges and needn't reach their ends.
All inputs are finite; a program needn't handle non-finite values.
Results may differ from the reference program's by a relative error of at most 0.02.
Values may be sent and summed in bfloat16 or wider, within the bound.
A program may use at most 128 MiB of HBM per device.

```python
import jax
import jax.numpy as jnp
from jax import lax

ALIGN_FEATURES = 256
HEAD_TOTAL = 8
HEAD_WIDTH = 32
FACTOR_FEATURES = 32
PAIR = 128
ALIGNED_ROWS = 256
CHAIN_LENGTH = 1024


def common_keys(key):
    return jnp.clip(jax.random.normal(key, (ALIGN_FEATURES, HEAD_TOTAL * HEAD_WIDTH), jnp.float32), -5.0, 5.0) * ALIGN_FEATURES ** (-0.5)


def draw_lookup_weights(key, part):
    shared = common_keys(key)
    return shared.astype(jnp.bfloat16)


def draw_probe_weights(key, part):
    key = jax.random.fold_in(key, 23)
    renewed_state = jnp.clip(jax.random.normal(key, (ALIGN_FEATURES, HEAD_TOTAL * HEAD_WIDTH), jnp.float32), -5.0, 5.0) * ALIGN_FEATURES ** (-0.5)
    return renewed_state.astype(jnp.bfloat16)


def shard_levels(stream_key, dims, cuts, smallest, high):
    def one(position, blocks):
        steps = jax.random.uniform(jax.random.fold_in(jax.random.fold_in(stream_key, 6), position), (blocks,), jnp.float32, smallest / len(cuts), high / len(cuts))
        return jnp.repeat(jnp.exp(steps), dims[position] // blocks).reshape((-1,) + (1,) * (len(dims) - position - 1))

    factor_of = one(*cuts[0])
    for cut in cuts[1:]:
        factor_of = factor_of * one(*cut)
    return factor_of


def scatter_about(own_key, extent, scale, most, pieces=(), dtype=jnp.bfloat16):
    array = jax.random.normal(own_key, extent, jnp.float32) * scale
    if len(pieces) > 0:
        array = shard_levels(own_key, extent, pieces, -0.22, 0.18) * array
    return jnp.clip(array, min=-most, max=most).astype(dtype)


def setup_inputs(seed: int = 0) -> dict:
    seeds = jax.random.split(jax.random.key(seed), 17)
    return {
        "alignment_embedding": scatter_about(seeds[0], (ALIGNED_ROWS, CHAIN_LENGTH, ALIGN_FEATURES), 1.0, 6.0, ((0, 16), (1, 32))),
        "heed_layer_gain": jnp.clip(1.0 + 0.15 * jax.random.normal(seeds[1], (ALIGN_FEATURES,), jnp.float32), 0.25, 1.75),
        "heed_layer_shift": scatter_about(seeds[2], (ALIGN_FEATURES,), 0.3, 1.75, (), jnp.float32),
        "probe_weights": draw_probe_weights(jax.random.fold_in(seeds[16], 71), 0),
        "lookup_weights": draw_lookup_weights(jax.random.fold_in(seeds[16], 71), 0),
        "content_weights": scatter_about(seeds[5], (ALIGN_FEATURES, HEAD_TOTAL * HEAD_WIDTH), ALIGN_FEATURES ** -0.5, 0.375),
        "sigmoid_weights": scatter_about(seeds[6], (ALIGN_FEATURES, HEAD_TOTAL * HEAD_WIDTH), ALIGN_FEATURES ** -0.5, 0.375),
        "sigmoid_shift": scatter_about(seeds[7], (HEAD_TOTAL * HEAD_WIDTH,), 1.0, 6.0, (), jnp.float32),
        "final_weights": scatter_about(seeds[8], (HEAD_TOTAL * HEAD_WIDTH, ALIGN_FEATURES), 0.25, 1.5),
        "final_shift": scatter_about(seeds[9], (ALIGN_FEATURES,), 0.3, 1.75, (), jnp.float32),
        "tensor_layer_gain": jnp.clip(1.0 + 0.15 * jax.random.normal(seeds[10], (ALIGN_FEATURES,), jnp.float32), 0.25, 1.75),
        "tensor_layer_shift": scatter_about(seeds[11], (ALIGN_FEATURES,), 0.3, 1.75, (), jnp.float32),
        "first_factor_weights": scatter_about(seeds[12], (ALIGN_FEATURES, FACTOR_FEATURES), ALIGN_FEATURES ** -0.5, 0.375),
        "second_factor_weights": scatter_about(seeds[13], (ALIGN_FEATURES, FACTOR_FEATURES), ALIGN_FEATURES ** -0.5, 0.375),
        "couple_weights": scatter_about(seeds[14], (FACTOR_FEATURES * FACTOR_FEATURES, PAIR), 0.5, 3.0),
        "couple_shift": scatter_about(seeds[15], (PAIR,), 0.3, 1.75, (), jnp.float32),
    }


def layer_norm(values, scale, offset):
    center = values - lax.optimization_barrier(jnp.mean(values, axis=-1, keepdims=True))
    spread = lax.optimization_barrier(jnp.mean(center * center, axis=-1, keepdims=True))
    return center * lax.rsqrt(spread + 1e-05) * scale + offset

def reference(alignment_embedding, heed_layer_gain, heed_layer_shift, probe_weights, lookup_weights, content_weights, sigmoid_weights, sigmoid_shift, final_weights, final_shift, tensor_layer_gain, tensor_layer_shift, first_factor_weights, second_factor_weights, couple_weights, couple_shift):
    given_tensor = alignment_embedding.astype(jnp.float32)
    standardized = layer_norm(given_tensor, heed_layer_gain, heed_layer_shift).astype(jnp.bfloat16)
    feature_tile = 16

    def position_tile(block):
        rows = block.shape[1]
        queries = jnp.dot(block, probe_weights, preferred_element_type=jnp.float32).astype(jnp.bfloat16)
        keys = jnp.dot(block, lookup_weights, preferred_element_type=jnp.float32).astype(jnp.bfloat16)
        values = jnp.dot(block, content_weights, preferred_element_type=jnp.float32).astype(jnp.bfloat16)
        queries = queries.reshape(ALIGNED_ROWS, rows, HEAD_TOTAL, HEAD_WIDTH).astype(jnp.float32)
        keys = keys.reshape(ALIGNED_ROWS, rows, HEAD_TOTAL, HEAD_WIDTH).astype(jnp.float32)
        values = values.reshape(ALIGNED_ROWS, rows, HEAD_TOTAL, HEAD_WIDTH).astype(jnp.float32)
        scores = jnp.einsum('srhd,trhd->rhst', queries, keys) / jnp.sqrt(jnp.float32(HEAD_WIDTH))
        weights = jax.nn.softmax(scores, axis=-1).astype(jnp.bfloat16)
        mixed = jnp.einsum('rhst,trhd->srhd', weights.astype(jnp.float32), values).reshape(ALIGNED_ROWS, rows, HEAD_TOTAL * HEAD_WIDTH)
        gate = jax.nn.sigmoid(jnp.dot(block, sigmoid_weights, preferred_element_type=jnp.float32) + sigmoid_shift)
        gated = (mixed * gate).astype(jnp.bfloat16)
        return (jnp.dot(gated, final_weights, preferred_element_type=jnp.float32) + final_shift).astype(jnp.bfloat16)
    tile_groups = standardized.reshape(ALIGNED_ROWS, CHAIN_LENGTH // feature_tile, feature_tile, ALIGN_FEATURES).transpose(1, 0, 2, 3)
    weighted_mixture = lax.map(position_tile, tile_groups).transpose(1, 0, 2, 3).reshape(ALIGNED_ROWS, CHAIN_LENGTH, ALIGN_FEATURES)
    updated = (given_tensor + weighted_mixture.astype(jnp.float32)).astype(jnp.bfloat16)
    outer_normed = layer_norm(updated.astype(jnp.float32), tensor_layer_gain, tensor_layer_shift).astype(jnp.bfloat16)
    left = jnp.dot(outer_normed, first_factor_weights, preferred_element_type=jnp.float32).astype(jnp.bfloat16)
    right = jnp.dot(outer_normed, second_factor_weights, preferred_element_type=jnp.float32).astype(jnp.bfloat16)
    right_flat = right.reshape(ALIGNED_ROWS, CHAIN_LENGTH * FACTOR_FEATURES)
    row_block = 8
    left_blocks = left.reshape(ALIGNED_ROWS, CHAIN_LENGTH // row_block, row_block * FACTOR_FEATURES).transpose(1, 0, 2)

    def pair_rows(piece):
        outer = lax.dot_general(piece, right_flat, (((0,), (0,)), ((), ())), preferred_element_type=jnp.float32)
        outer = (outer / ALIGNED_ROWS).astype(jnp.bfloat16)
        outer = outer.reshape(row_block, FACTOR_FEATURES, CHAIN_LENGTH, FACTOR_FEATURES).transpose(0, 2, 1, 3).reshape(row_block, CHAIN_LENGTH, FACTOR_FEATURES * FACTOR_FEATURES)
        return (jnp.dot(outer, couple_weights, preferred_element_type=jnp.float32) + couple_shift).astype(jnp.bfloat16)
    pair_update = lax.map(pair_rows, left_blocks).reshape(CHAIN_LENGTH, CHAIN_LENGTH, PAIR)
    return (updated, pair_update)
```

```python
import functools

import jax
import jax.numpy as jnp
from jax import lax
from jax.experimental import pallas as pl
from jax.experimental.pallas import tpu as pltpu
from jax.sharding import PartitionSpec as P

HEADS = 8
WIDTH = 32
BF16 = jnp.bfloat16
F32 = jnp.float32
MESH = pl.DeviceIdType.MESH
SPREAD = (4, 5, 3, 6, 2, 7, 1)


def norm_rows(values, scale, offset):
    center = values - jnp.mean(values, axis=-1, keepdims=True)
    spread = jnp.mean(center * center, axis=-1, keepdims=True)
    return center * lax.rsqrt(spread + 1e-05) * scale + offset


def dot(a, b):
    return jnp.dot(a, b, preferred_element_type=F32)


def dot_t(a, b):
    return lax.dot_general(a, b, (((1,), (1,)), ((), ())), preferred_element_type=F32)


def relay_of(p, y, zl):
    x, zh = p // 4, p % 4
    y_to, zl_to = p // 2, p % 2
    k = (y - y_to + 12) % 8
    dx = (2 * (k // 4) + 3 * (k % 2)) % 4
    far = ((k + 2) // 4) % 2
    e = (zl + zl_to) % 2
    s = 2 * zl_to - 1
    dz = (1 - e) * far * s + e * (far * 2 - (1 - far) * s)
    return (x + dx) % 4, (zh + dz + 8) % 4


def chunk_at(p, x, zh):
    x0, zh0 = p // 4, p % 4
    zl_to = p % 2
    s = 2 * zl_to - 1
    w = (x0 - x + 4) % 4
    u = ((zh - zh0 + 4) * (s + 4)) % 4
    e = u // 2
    far = ((u + 1) // 2) % 2
    k = w + (1 - far) * 4 * (w // 2) + 2 * far
    return (p // 2 + k + 4) % 8, (e + zl_to) % 2


def kernel(
    x_hbm, gain1, shift1, wq_hbm, wk_hbm, wv_hbm, wg_hbm, bg, wf_hbm, bf, gain2, shift2,
    w1_hbm, w2_hbm, wc_hbm, bc,
    upd_out, pair_out,
    xv, x32, xt, xg, wq, wk, wv, wg, wf, w1, w2, wc, w32, wt, w12t, vtx, gated_t, bd,
    upd, upd_all, lt, rt, left, right, r32, right_p, outer, pair,
    load_sem, a_send, a_recv, u_send, u_recv, p_send, p_recv, ry_send, ry_recv, rz_send, rz_recv,
    lz_send, lz_recv, lx_send, lx_recv, lc_send, lc_recv,
):
    q = lax.axis_index("seq")
    r = lax.axis_index("res")
    y, zl = q // 2, q % 2
    x, zh, c = r // 8, (r // 2) % 4, r % 2
    plane = r // 2

    def res(x_, zh_, c_):
        return (x_ * 4 + zh_) * 2 + c_

    def send(src, dst, ss, rs, dev):
        copy = pltpu.make_async_remote_copy(
            src_ref=src, dst_ref=dst, send_sem=ss, recv_sem=rs, device_id=dev, device_id_type=MESH
        )
        return copy

    seq_dev = [((q + k) % 16, r) for k in range(16)]
    y_dev = [(((y + k) % 8) * 2 + zl, r) for k in range(8)]
    zl_dev = (y * 2 + 1 - zl, r)
    zh_dev = [(q, res(x, (zh + k) % 4, c)) for k in range(4)]
    x_dev = [(q, res((x + k) % 4, zh, c)) for k in range(4)]
    core_dev = (q, res(x, zh, 1 - c))
    relay_x, relay_zh = relay_of(plane, y, zl)
    relay_dev = (plane, res(relay_x, relay_zh, c))
    from_y, from_zl = chunk_at(q, x, zh)
    from_dev = (from_y * 2 + from_zl, 2 * q + c)

    barrier = pltpu.get_barrier_semaphore()
    greet = seq_dev[1:] + zh_dev[1:] + x_dev[1:] + [core_dev, from_dev]
    for dev in greet:
        pl.semaphore_signal(barrier, inc=1, device_id=dev, device_id_type=MESH)

    loads = [
        pltpu.make_async_copy(a, b, load_sem.at[i])
        for i, (a, b) in enumerate(
            [(x_hbm, xv), (wc_hbm, wc), (wq_hbm, wq), (wk_hbm, wk), (wv_hbm, wv), (wg_hbm, wg),
             (wf_hbm, wf), (w1_hbm, w1), (w2_hbm, w2)]
        )
    ]
    for copy in loads:
        copy.start()

    loads[0].wait()

    @pl.loop(0, 16)
    def _(i):
        for half in range(2):
            x32[half, pl.ds(pl.multiple_of(i * 32, 32), 32), :] = xv[i, :, half * 128:(half + 1) * 128].astype(F32)

    @pl.loop(0, 32)
    def _(i):
        for half in range(2):
            xt[i, :, half * 128:(half + 1) * 128] = x32[half, pl.ds(i, 16, stride=32), :].astype(BF16)

    mine = pl.ds(pl.multiple_of(q * 16, 16), 16)
    for m in range(2):
        xg[m, mine, :] = xt[2 * q + m]

    pl.semaphore_wait(barrier, len(greet))
    order = (8, 7, 9, 6, 10, 5, 11, 4, 12, 3, 13, 2, 14, 1, 15)
    turn = {}
    for k in order:
        to = seq_dev[k][0]
        turn[k] = send(xt.at[pl.ds(2 * to, 2)], xg.at[:, mine, :], a_send.at[k], a_recv.at[k], seq_dev[k])
        turn[k].start()

    for copy in loads[1:]:
        copy.wait()
    wt[0:256, :] = wq[...].astype(F32).T.astype(BF16)
    wt[256:512, :] = wv[...].astype(F32).T.astype(BF16)
    wt[512:768, :] = wg[...].astype(F32).T.astype(BF16)
    w12t[0:32, :] = w1[...].astype(F32).T.astype(BF16)
    w12t[32:64, :] = w2[...].astype(F32).T.astype(BF16)
    vtx[:, 32:48, :] = jnp.ones((HEADS, 16, 256), BF16)
    w32[...] = wc[...].astype(F32)

    @pl.loop(0, 32)
    def _(b):
        block = w32[pl.ds(b, 32, stride=32), :].astype(BF16)
        zero = jnp.zeros((32, 128), BF16)
        for i in range(4):
            rows = pl.ds(pl.multiple_of(b * 128 + i * 32, 32), 32)
            for j in range(4):
                bd[rows, j * 128:(j + 1) * 128] = block if i == j else zero

    for k in order[::-1]:
        turn[k].wait_recv()

    for m in range(2):
        given = xg[m].astype(F32)
        normed = norm_rows(given, gain1[...], shift1[...]).astype(BF16)
        keys = dot(normed, wk[...]).astype(BF16)
        qvg = dot_t(wt[...], normed)
        queries_t = qvg[0:256].astype(BF16)
        vtx[:, 0:32, :] = qvg[256:512].astype(BF16).reshape(HEADS, WIDTH, 256)
        gate_t = 1.0 / (1.0 + jnp.exp(-(qvg[512:768] + bg[...])))
        for h in range(HEADS):
            span = slice(h * WIDTH, (h + 1) * WIDTH)
            scores = dot(keys[:, span], queries_t[span, :])
            top = jnp.max(scores, axis=0, keepdims=True)
            weights = jnp.exp((scores - top) * (1.0 / 32.0 ** 0.5)).astype(BF16)
            mixed = dot(vtx[h], weights)
            gated_t[span, :] = mixed[0:32] * (1.0 / mixed[32:33]) * gate_t[span, :]
        gated = gated_t[...].T.astype(BF16)
        attended = (dot(gated, wf[...]) + bf[...]).astype(BF16)
        updated = (given + attended.astype(F32)).astype(BF16)
        upd[m] = updated
        outer_normed = norm_rows(updated.astype(F32), gain2[...], shift2[...]).astype(BF16)
        both = dot_t(w12t[...], outer_normed).astype(BF16)
        lt[m * 32:(m + 1) * 32, :] = both[0:32]
        rt[m * 32:(m + 1) * 32, :] = both[32:64]

    def left_chunk(c_, y_, zl_):
        return left.at[c_ * 8 + y_, pl.ds(pl.multiple_of(zl_ * 64, 64), 64)]

    sent = []

    def go(*args):
        copy = send(*args)
        copy.start()
        sent.append(copy)
        return copy

    relay = go(lt, left_chunk(c, y, zl), p_send.at[0], p_recv.at[0], relay_dev)
    across = [go(rt, right.at[q], rz_send.at[0], rz_recv.at[0], zl_dev)]
    along = [None] * 8
    for k in SPREAD[::-1]:
        along[k] = go(rt, right.at[q], ry_send.at[k], ry_recv.at[k], y_dev[k])
    right[q] = rt[...]
    back = []
    for k in order:
        to = seq_dev[k][0]
        back.append(
            go(upd.at[:, pl.ds(pl.multiple_of(to * 16, 16), 16), :], upd_all.at[pl.ds(2 * q, 2)],
               u_send.at[k], u_recv.at[k], seq_dev[k])
        )
    for m in range(2):
        upd_all[2 * q + m] = upd[m, mine, :]

    def pass_on(cy, czl, i):
        here = left_chunk(c, cy, czl)
        xs = [go(here, here, lx_send.at[i * 3 + k - 1], lx_recv.at[i * 3 + k - 1], x_dev[k]) for k in (2, 1, 3)]
        go(here, here, lc_send.at[i], lc_recv.at[i], core_dev)
        return xs

    relay.wait_recv()
    here = left_chunk(c, from_y, from_zl)
    zs = {k: go(here, here, lz_send.at[k - 1], lz_recv.at[k - 1], zh_dev[k]) for k in (2, 1, 3)}
    pass_on(from_y, from_zl, 0)
    for k in SPREAD[::-1]:
        along[k].wait_recv()
        slot = ((y + 8 - k) % 8) * 2 + zl
        across.append(go(right.at[slot], right.at[slot], rz_send.at[k], rz_recv.at[k], zl_dev))
    for k in (1, 3, 2):
        zs[k].wait_recv()
        cy, czl = chunk_at(q, x, (zh + 4 - k) % 4)
        pass_on(cy, czl, k)
    for copy in across:
        copy.wait_recv()

    @pl.loop(0, 16)
    def _(i):
        for half in range(2):
            r32[half, pl.ds(pl.multiple_of(i * 64, 64), 64), :] = right[i, :, half * 128:(half + 1) * 128].astype(F32)

    @pl.loop(0, 32)
    def _(b):
        rows = pl.ds(pl.multiple_of(b * 32, 32), 32)
        for half in range(2):
            right_p[rows, half * 128:(half + 1) * 128] = r32[half, pl.ds(b, 32, stride=32), :].astype(BF16)

    def outer_of(c_, x_):
        ya, _ = chunk_at(q, x_, zh)
        yb, _ = chunk_at(q, x_, (zh + 1) % 4)
        yc, _ = chunk_at(q, x_, (zh + 2) % 4)
        y2 = jnp.where(yb == ya, yc, yb)
        ga, gb = c_ * 8 + ya, c_ * 8 + y2
        rows = jnp.concatenate([left[ga], left[gb]], axis=0)

        @pl.loop(0, 4)
        def _(t):
            part = dot_t(right_p[pl.ds(pl.multiple_of(t * 256, 256), 256), :], rows).astype(BF16)
            for b in range(8):
                lanes = pl.ds(pl.multiple_of(t * 1024 + b * 128, 128), 128)
                outer[ga, :, lanes] = part[b * 32:(b + 1) * 32, 0:128]
                outer[gb, :, lanes] = part[b * 32:(b + 1) * 32, 128:256]

    def pair_of(c_):
        @pl.loop(0, 2)
        def _(t):
            first = c_ * 8 + t * 4
            rows = outer[pl.ds(first, 4)].reshape(128, 4096)
            total = dot(rows, bd[...]) * (1.0 / 256.0)
            for g in range(4):
                for i in range(4):
                    pair[(first + g) * 4 + i] = (
                        total[g * 32:(g + 1) * 32, i * 128:(i + 1) * 128] + bc[...]
                    ).astype(BF16)

    outer_of(c, x)
    for k in (1, 3, 2):
        xo = (x + 4 - k) % 4
        for i in range(4):
            cy, czl = chunk_at(q, xo, (zh + 4 - i) % 4)
            here = left_chunk(c, cy, czl)
            send(here, here, lx_send.at[i * 3 + k - 1], lx_recv.at[i * 3 + k - 1], x_dev[k]).wait_recv()
            go(here, here, lc_send.at[4 + (k - 1) * 4 + i], lc_recv.at[4 + (k - 1) * 4 + i], core_dev)
        outer_of(c, xo)
    pair_of(c)
    for k in (0, 1, 3, 2):
        xo = (x + 4 - k) % 4
        for i in range(4):
            cy, czl = chunk_at(q, xo, (zh + 4 - i) % 4)
            there = left_chunk(1 - c, cy, czl)
            slot = i if k == 0 else 4 + (k - 1) * 4 + i
            send(there, there, lc_send.at[slot], lc_recv.at[slot], core_dev).wait_recv()
        outer_of(1 - c, xo)
    pair_of(1 - c)

    out1 = pltpu.make_async_copy(pair, pair_out, load_sem.at[0])
    out1.start()
    for copy in back:
        copy.wait_recv()
    out2 = pltpu.make_async_copy(upd_all, upd_out, load_sem.at[1])
    out2.start()
    for k in order:
        turn[k].wait_send()
    for copy in sent:
        copy.wait_send()
    out1.wait()
    out2.wait()


def local(
    alignment_embedding, heed_layer_gain, heed_layer_shift, probe_weights, lookup_weights,
    content_weights, sigmoid_weights, sigmoid_shift, final_weights, final_shift,
    tensor_layer_gain, tensor_layer_shift, first_factor_weights, second_factor_weights,
    couple_weights, couple_shift,
):
    row = lambda a: a.reshape(1, -1)
    hbm = pl.BlockSpec(memory_space=pl.ANY)
    vmem = pl.BlockSpec(memory_space=pltpu.VMEM)
    sem = pltpu.SemaphoreType.DMA
    buf = lambda *shape: pltpu.VMEM(shape, BF16)
    upd, pair = pl.pallas_call(
        kernel,
        out_shape=(
            jax.ShapeDtypeStruct((32, 16, 256), BF16),
            jax.ShapeDtypeStruct((64, 32, 128), BF16),
        ),
        in_specs=[hbm, vmem, vmem, hbm, hbm, hbm, hbm, vmem, hbm, vmem, vmem, vmem, hbm, hbm, hbm, vmem],
        out_specs=(hbm, hbm),
        scratch_shapes=[
            buf(16, 32, 256), pltpu.VMEM((2, 512, 128), F32), buf(32, 16, 256), buf(2, 256, 256),
            buf(256, 256), buf(256, 256), buf(256, 256), buf(256, 256), buf(256, 256),
            buf(256, 32), buf(256, 32), buf(1024, 128), pltpu.VMEM((1024, 128), F32),
            buf(768, 256), buf(64, 256), buf(8, 48, 256), pltpu.VMEM((256, 256), F32), buf(4096, 512),
            buf(2, 256, 256), buf(32, 16, 256), buf(64, 256), buf(64, 256), buf(16, 128, 256),
            buf(16, 64, 256), pltpu.VMEM((2, 1024, 128), F32), buf(1024, 256), buf(16, 32, 4096),
            buf(64, 32, 128),
            sem((9,)), sem((16,)), sem((16,)), sem((16,)), sem((16,)), sem((1,)), sem((1,)),
            sem((8,)), sem((8,)), sem((8,)), sem((8,)), sem((3,)), sem((3,)),
            sem((12,)), sem((12,)), sem((16,)), sem((16,)),
        ],
        compiler_params=pltpu.CompilerParams(
            collective_id=0, has_side_effects=True, vmem_limit_bytes=40 * 2**20
        ),
        name="evoformer",
    )(
        alignment_embedding, row(heed_layer_gain), row(heed_layer_shift), probe_weights,
        lookup_weights, content_weights, sigmoid_weights, sigmoid_shift.reshape(-1, 1),
        final_weights, row(final_shift), row(tensor_layer_gain), row(tensor_layer_shift),
        first_factor_weights, second_factor_weights, couple_weights, row(couple_shift),
    )
    return upd.transpose(1, 0, 2), pair


def solution(mesh):
    return jax.shard_map(
        local,
        mesh=mesh,
        in_specs=(P("seq", "res", None),) + (P(),) * 15,
        out_specs=(P("seq", "res", None), P("seq", "res", None)),
        check_vma=False,
    )
```

```python
import functools

import jax
import jax.numpy as jnp
from jax import lax
from jax.experimental import pallas as pl
from jax.experimental.pallas import tpu as pltpu
from jax.sharding import PartitionSpec as P

HEADS = 8
WIDTH = 32
BF16 = jnp.bfloat16
F32 = jnp.float32
MESH = pl.DeviceIdType.MESH
SPREAD = (4, 5, 3, 6, 2, 7, 1)
SCALE = 1.4426950408889634 / 32.0**0.5


def norm_rows(values, scale, offset):
    center = values - jnp.mean(values, axis=-1, keepdims=True)
    spread = jnp.mean(center * center, axis=-1, keepdims=True)
    return center * lax.rsqrt(spread + 1e-05) * scale + offset


def dot(a, b):
    return jnp.dot(a, b, preferred_element_type=F32)


def dot_t(a, b):
    return lax.dot_general(a, b, (((1,), (1,)), ((), ())), preferred_element_type=F32)


def relay_of(p, y, zl):
    x, zh = p // 4, p % 4
    y_to, zl_to = p // 2, p % 2
    k = (y - y_to + 12) % 8
    dx = (2 * (k // 4) + 3 * (k % 2)) % 4
    far = ((k + 2) // 4) % 2
    e = (zl + zl_to) % 2
    s = 2 * zl_to - 1
    dz = (1 - e) * far * s + e * (far * 2 - (1 - far) * s)
    return (x + dx) % 4, (zh + dz + 8) % 4


def chunk_at(p, x, zh):
    x0, zh0 = p // 4, p % 4
    zl_to = p % 2
    s = 2 * zl_to - 1
    w = (x0 - x + 4) % 4
    u = ((zh - zh0 + 4) * (s + 4)) % 4
    e = u // 2
    far = ((u + 1) // 2) % 2
    k = w + (1 - far) * 4 * (w // 2) + 2 * far
    return (p // 2 + k + 4) % 8, (e + zl_to) % 2


def kernel(
    x_hbm, gain1_hbm, shift1_hbm, wq_hbm, wk_hbm, wv_hbm, wg_hbm, bg_hbm, wf_hbm, bf_hbm, gain2_hbm,
    shift2_hbm, w1_hbm, w2_hbm, wc_hbm, bc_hbm,
    upd_out, pair_out,
    xv, x32, xt, xg, gain1, shift1, bg, bf, gain2, shift2, bc, wq, wk, wv, wg, wf, w12t, wc, w32,
    wt, bg_t, vtx, gated_t, bd,
    upd, upd_all, upd_v, lt, rt, left, right, r32, right_p, outer, pair,
    load_sem, a_send, a_recv, u_send, u_recv, p_send, p_recv, ry_send, ry_recv, rz_send, rz_recv,
    lz_send, lz_recv, lx_send, lx_recv, lc_send, lc_recv,
):
    q = lax.axis_index("seq")
    r = lax.axis_index("res")
    y, zl = q // 2, q % 2
    x, zh, c = r // 8, (r // 2) % 4, r % 2
    plane = r // 2

    def res(x_, zh_, c_):
        return (x_ * 4 + zh_) * 2 + c_

    sent = []

    def copy_to(dev, src, dst, ss, rs, i):
        return pltpu.make_async_remote_copy(
            src_ref=src, dst_ref=dst, send_sem=ss.at[i], recv_sem=rs.at[i], device_id=dev,
            device_id_type=MESH,
        )

    def go(*args):
        copy = copy_to(*args)
        copy.start()
        sent.append(copy)
        return copy

    seq_dev = [((q + k) % 16, r) for k in range(16)]
    y_dev = [(((y + k) % 8) * 2 + zl, r) for k in range(8)]
    zl_dev = (y * 2 + 1 - zl, r)
    zh_dev = [(q, res(x, (zh + k) % 4, c)) for k in range(4)]
    x_dev = [(q, res((x + k) % 4, zh, c)) for k in range(4)]
    core_dev = (q, res(x, zh, 1 - c))
    relay_x, relay_zh = relay_of(plane, y, zl)
    relay_dev = (plane, res(relay_x, relay_zh, c))
    source = [[chunk_at(q, (x + 4 - i) % 4, (zh + 4 - j) % 4) for j in range(4)] for i in range(4)]
    held = [[source[i][j][0] * 2 + source[i][j][1] for j in range(4)] for i in range(4)]
    from_dev = (held[0][0], 2 * q + c)

    barrier = pltpu.get_barrier_semaphore()
    greet = seq_dev[1:] + zh_dev[1:] + x_dev[1:] + [core_dev, from_dev]
    for dev in greet:
        pl.semaphore_signal(barrier, inc=1, device_id=dev, device_id_type=MESH)

    loads = [
        pltpu.make_async_copy(a, b, load_sem.at[i])
        for i, (a, b) in enumerate(
            [(x_hbm, xv), (wc_hbm, wc), (wq_hbm, wq), (wk_hbm, wk), (wv_hbm, wv), (wg_hbm, wg),
             (wf_hbm, wf), (w1_hbm, w12t.at[0:32]), (w2_hbm, w12t.at[32:64]), (gain1_hbm, gain1),
             (shift1_hbm, shift1), (bg_hbm, bg), (bf_hbm, bf), (gain2_hbm, gain2),
             (shift2_hbm, shift2), (bc_hbm, bc)]
        )
    ]
    for copy in loads:
        copy.start()

    loads[0].wait()
    for i in range(16):
        for half in range(2):
            x32[half, i * 32:(i + 1) * 32, :] = xv[i, :, half * 128:(half + 1) * 128].astype(F32)
    for i in range(32):
        for half in range(2):
            xt[i, :, half * 128:(half + 1) * 128] = x32[half, pl.ds(i, 16, stride=32), :].astype(BF16)

    mine = pl.ds(pl.multiple_of(q * 16, 16), 16)
    for m in range(2):
        xg[m, mine, :] = xt[2 * q + m]

    pl.semaphore_wait(barrier, len(greet))
    order = (8, 7, 9, 6, 10, 5, 11, 4, 12, 3, 13, 2, 14, 1, 15)
    turn = [
        [go(seq_dev[k], xt.at[2 * seq_dev[k][0] + m], xg.at[m, mine, :], a_send, a_recv, m * 16 + k)
         for k in order]
        for m in range(2)
    ]

    for copy in loads[1:]:
        copy.wait()
    wt[0:256, :] = wq[...].astype(F32).T.astype(BF16)
    wt[256:512, :] = wv[...].astype(F32).T.astype(BF16)
    wt[512:768, :] = wg[...].astype(F32).T.astype(BF16)
    bg_t[...] = jnp.broadcast_to(bg[...], (128, 256)).T
    vtx[:, 32:48, :] = jnp.ones((HEADS, 16, 256), BF16)
    w32[...] = wc[...].astype(F32)

    @pl.loop(0, 32)
    def _(b):
        block = w32[pl.ds(b, 32, stride=32), :].astype(BF16)
        zero = jnp.zeros((32, 128), BF16)
        for i in range(4):
            rows = pl.ds(pl.multiple_of(b * 128 + i * 32, 32), 32)
            for j in range(4):
                bd[rows, j * 128:(j + 1) * 128] = block if i == j else zero

    def attend(m):
        given = xg[m].astype(F32)
        normed = norm_rows(given, gain1[...], shift1[...]).astype(BF16)
        keys = dot(normed, wk[...]).astype(BF16)
        qvg = dot_t(wt[...], normed)
        queries_t = qvg[0:256].astype(BF16)
        vtx[:, 0:32, :] = qvg[256:512].astype(BF16).reshape(HEADS, WIDTH, 256)
        gate_t = 1.0 / (1.0 + jnp.exp(-(qvg[512:768] + bg_t[:, 0:1])))
        for h in range(HEADS):
            span = slice(h * WIDTH, (h + 1) * WIDTH)
            scores = dot(keys[:, span], queries_t[span, :])
            top = jnp.max(scores, axis=0, keepdims=True)
            weights = jnp.exp2((scores - top) * SCALE).astype(BF16)
            mixed = dot(vtx[h], weights)
            gated_t[span, :] = mixed[0:32] * (1.0 / mixed[32:33]) * gate_t[span, :]
        gated = gated_t[...].T.astype(BF16)
        attended = (dot(gated, wf[...]) + bf[...]).astype(BF16)
        updated = (given + attended.astype(F32)).astype(BF16)
        upd[m] = updated
        outer_normed = norm_rows(updated.astype(F32), gain2[...], shift2[...]).astype(BF16)
        both = dot_t(w12t[...], outer_normed).astype(BF16)
        lt[m] = both[0:32]
        rt[m] = both[32:64]

    def slot(c_, q_, m):
        return left.at[(c_ * 16 + q_) * 2 + m]

    relay, along, across, back = [], [], [], []
    for m in range(2):
        for copy in turn[m][::-1]:
            copy.wait_recv()
        attend(m)
        relay.append(go(relay_dev, lt.at[m], slot(c, q, m), p_send, p_recv, m))
        here = right.at[2 * q + m]
        across.append(go(zl_dev, rt.at[m], here, rz_send, rz_recv, m * 8))
        along.append(
            {k: go(y_dev[k], rt.at[m], here, ry_send, ry_recv, m * 8 + k) for k in SPREAD}
        )
        right[2 * q + m] = rt[m]
        for k in order:
            rows = pl.ds(pl.multiple_of(seq_dev[k][0] * 16, 16), 16)
            back.append(
                go(seq_dev[k], upd.at[m, rows, :], upd_all.at[2 * q + m], u_send, u_recv, m * 16 + k)
            )
        upd_all[2 * q + m] = upd[m, mine, :]

    def pass_on(j, m):
        here = slot(c, held[0][j], m)
        for k in (2, 1, 3):
            go(x_dev[k], here, here, lx_send, lx_recv, m * 12 + j * 3 + k - 1)
        go(core_dev, here, here, lc_send, lc_recv, m * 16 + j)

    z_left = []
    for m in range(2):
        relay[m].wait_recv()
        here = slot(c, held[0][0], m)
        z_left.append({k: go(zh_dev[k], here, here, lz_send, lz_recv, m * 3 + k - 1) for k in (2, 1, 3)})
        pass_on(0, m)
        for k in SPREAD[::-1]:
            along[m][k].wait_recv()
            here = right.at[(((y + 8 - k) % 8) * 2 + zl) * 2 + m]
            across.append(go(zl_dev, here, here, rz_send, rz_recv, m * 8 + k))
    for m in range(2):
        for k in (1, 3, 2):
            z_left[m][k].wait_recv()
            pass_on(k, m)

    for copy in across:
        copy.wait_recv()

    for i in range(32):
        for half in range(2):
            r32[half, i * 32:(i + 1) * 32, :] = right[i, :, half * 128:(half + 1) * 128].astype(F32)
    for b in range(32):
        for half in range(2):
            right_p[b * 32:(b + 1) * 32, half * 128:(half + 1) * 128] = r32[
                half, pl.ds(b, 32, stride=32), :
            ].astype(BF16)

    def outer_of(c_, m, pick):
        at = [(c_ * 16 + held[i][j]) * 2 + m for i, j in pick]
        rows = jnp.concatenate([left[n] for n in at], axis=0)
        for t in range(4):
            part = dot_t(right_p[t * 256:(t + 1) * 256, :], rows).astype(BF16)
            for b in range(8):
                lanes = slice(t * 1024 + b * 128, t * 1024 + (b + 1) * 128)
                for g in range(2):
                    outer[group_no[0] * 2 + g, :, lanes] = part[b * 32:(b + 1) * 32, g * 128:(g + 1) * 128]
        owner.extend(c_ * 32 + 2 * held[i][j] + m for i, j in pick)
        group_no[0] += 1

    group_no, owner = [0], []

    def pair_of(first, count):
        rows = outer[first:first + count].reshape(count * 32, 4096)
        total = dot(rows, bd[...]) * (1.0 / 256.0)
        for g in range(count):
            for i in range(4):
                pair[owner[(first + g) * 4 + i]] = (
                    total[g * 32:(g + 1) * 32, i * 128:(i + 1) * 128] + bc[...]
                ).astype(BF16)

    FIRST = [(i, j) for j in (0, 1) for i in range(4)]
    SECOND = [(i, j) for j in (3, 2) for i in range(4)]

    def from_x(m):
        for j in (0, 1, 3, 2):
            for k in (1, 3, 2):
                here = slot(c, held[k][j], m)
                copy_to(x_dev[k], here, here, lx_send, lx_recv, m * 12 + j * 3 + k - 1).wait_recv()
                go(core_dev, here, here, lc_send, lc_recv, m * 16 + k * 4 + j)

    def from_core(m, pick):
        for k, j in pick:
            there = slot(1 - c, held[k][j], m)
            copy_to(core_dev, there, there, lc_send, lc_recv, m * 16 + k * 4 + j).wait_recv()

    from_x(0)
    outer_of(c, 0, FIRST)
    outer_of(c, 0, SECOND)

    for copy in back:
        copy.wait_recv()
    for i in range(32):
        for half in range(2):
            x32[half, i * 16:(i + 1) * 16, :] = upd_all[i, :, half * 128:(half + 1) * 128].astype(F32)
    for i in range(16):
        for half in range(2):
            upd_v[i, :, half * 128:(half + 1) * 128] = x32[half, pl.ds(i, 32, stride=16), :].astype(BF16)
    out1 = pltpu.make_async_copy(upd_v, upd_out, load_sem.at[0])
    out1.start()

    from_core(0, FIRST)
    outer_of(1 - c, 0, FIRST)
    from_core(0, SECOND)
    outer_of(1 - c, 0, SECOND)
    from_x(1)
    pair_of(0, 8)
    outer_of(c, 1, FIRST)
    outer_of(c, 1, SECOND)
    pair_of(8, 4)
    from_core(1, FIRST)
    outer_of(1 - c, 1, FIRST)
    from_core(1, SECOND)
    outer_of(1 - c, 1, SECOND)
    pair_of(12, 4)

    out2 = pltpu.make_async_copy(pair, pair_out, load_sem.at[1])
    out2.start()
    for copy in sent:
        copy.wait_send()
    out1.wait()
    out2.wait()


def local(
    alignment_embedding, heed_layer_gain, heed_layer_shift, probe_weights, lookup_weights,
    content_weights, sigmoid_weights, sigmoid_shift, final_weights, final_shift,
    tensor_layer_gain, tensor_layer_shift, first_factor_weights, second_factor_weights,
    couple_weights, couple_shift,
):
    row = lambda a: a.reshape(1, -1)
    hbm = pl.BlockSpec(memory_space=pltpu.HBM)
    sem = pltpu.SemaphoreType.DMA
    buf = lambda *shape: pltpu.VMEM(shape, BF16)
    line = lambda n: pltpu.VMEM((1, n), F32)
    upd, pair = pl.pallas_call(
        kernel,
        out_shape=(
            jax.ShapeDtypeStruct((16, 32, 256), BF16),
            jax.ShapeDtypeStruct((64, 32, 128), BF16),
        ),
        in_specs=[hbm] * 16,
        out_specs=(hbm, hbm),
        scratch_shapes=[
            buf(16, 32, 256), pltpu.VMEM((2, 512, 128), F32), buf(32, 16, 256), buf(2, 256, 256),
            line(256), line(256), line(256), line(256), line(256), line(256), line(128),
            buf(256, 256), buf(256, 256), buf(256, 256), buf(256, 256), buf(256, 256),
            buf(64, 256), buf(1024, 128), pltpu.VMEM((1024, 128), F32),
            buf(768, 256), pltpu.VMEM((256, 128), F32), buf(8, 48, 256), pltpu.VMEM((256, 256), F32), buf(4096, 512),
            buf(2, 256, 256), buf(32, 16, 256), buf(16, 32, 256), buf(2, 32, 256), buf(2, 32, 256),
            buf(64, 32, 256), buf(32, 32, 256), pltpu.VMEM((2, 1024, 128), F32), buf(1024, 256), buf(16, 32, 4096),
            buf(64, 32, 128),
            sem((16,)), sem((32,)), sem((32,)), sem((32,)), sem((32,)), sem((2,)), sem((2,)),
            sem((16,)), sem((16,)), sem((16,)), sem((16,)), sem((6,)), sem((6,)),
            sem((24,)), sem((24,)), sem((32,)), sem((32,)),
        ],
        compiler_params=pltpu.CompilerParams(
            collective_id=0, has_side_effects=True, vmem_limit_bytes=60 * 2**20
        ),
        name="evoformer",
    )(
        alignment_embedding, row(heed_layer_gain), row(heed_layer_shift), probe_weights,
        lookup_weights, content_weights, sigmoid_weights, row(sigmoid_shift),
        final_weights, row(final_shift), row(tensor_layer_gain), row(tensor_layer_shift),
        first_factor_weights.T, second_factor_weights.T, couple_weights, row(couple_shift),
    )
    return upd, pair


def solution(mesh):
    return jax.shard_map(
        local,
        mesh=mesh,
        in_specs=(P("seq", "res", None),) + (P(),) * 15,
        out_specs=(P("seq", "res", None), P("seq", "res", None)),
        check_vma=False,
    )
```

```python
import functools

import jax
import jax.numpy as jnp
from jax import lax
from jax.experimental import pallas as pl
from jax.experimental.pallas import tpu as pltpu
from jax.sharding import PartitionSpec as P

HEADS = 8
WIDTH = 32
BF16 = jnp.bfloat16
F32 = jnp.float32
MESH = pl.DeviceIdType.MESH
SPREAD = (4, 5, 3, 6, 2, 7, 1)
SCALE = 1.4426950408889634 / 32.0**0.5


def norm_rows(values, scale, offset):
    center = values - jnp.mean(values, axis=-1, keepdims=True)
    spread = jnp.mean(center * center, axis=-1, keepdims=True)
    return center * lax.rsqrt(spread + 1e-05) * scale + offset


def dot(a, b):
    return jnp.dot(a, b, preferred_element_type=F32)


def dot_t(a, b):
    return lax.dot_general(a, b, (((1,), (1,)), ((), ())), preferred_element_type=F32)


def relay_of(p, y, zl):
    x, zh = p // 4, p % 4
    y_to, zl_to = p // 2, p % 2
    k = (y - y_to + 12) % 8
    dx = (2 * (k // 4) + 3 * (k % 2)) % 4
    far = ((k + 2) // 4) % 2
    e = (zl + zl_to) % 2
    s = 2 * zl_to - 1
    dz = (1 - e) * far * s + e * (far * 2 - (1 - far) * s)
    return (x + dx) % 4, (zh + dz + 8) % 4


def chunk_at(p, x, zh):
    x0, zh0 = p // 4, p % 4
    zl_to = p % 2
    s = 2 * zl_to - 1
    w = (x0 - x + 4) % 4
    u = ((zh - zh0 + 4) * (s + 4)) % 4
    e = u // 2
    far = ((u + 1) // 2) % 2
    k = w + (1 - far) * 4 * (w // 2) + 2 * far
    return (p // 2 + k + 4) % 8, (e + zl_to) % 2


def kernel(
    x_hbm, gain1_hbm, shift1_hbm, wq_hbm, wk_hbm, wv_hbm, wg_hbm, bg_hbm, wf_hbm, bf_hbm, gain2_hbm,
    shift2_hbm, w1_hbm, w2_hbm, wc_hbm, bc_hbm,
    upd_v, pair,
    xv, x32, xt, xg, gain1, shift1, bg, bf, gain2, shift2, bc, wq, wk, wv, wg, wf, w12t, wc, w32,
    wt, bg_t, vtx, weights, gated_t, bd,
    upd, upd_all, lt, rt, left, right, r32, right_p, outer,
    load_sem, a_send, a_recv, u_send, u_recv, p_send, p_recv, ry_send, ry_recv, rz_send, rz_recv,
    lz_send, lz_recv, lx_send, lx_recv, lc_send, lc_recv,
):
    q = lax.axis_index("seq")
    r = lax.axis_index("res")
    y, zl = q // 2, q % 2
    x, zh, c = r // 8, (r // 2) % 4, r % 2
    plane = r // 2

    def res(x_, zh_, c_):
        return (x_ * 4 + zh_) * 2 + c_

    sent = []

    def copy_to(dev, src, dst, ss, rs, i):
        return pltpu.make_async_remote_copy(
            src_ref=src, dst_ref=dst, send_sem=ss.at[i], recv_sem=rs.at[i], device_id=dev,
            device_id_type=MESH,
        )

    def go(*args):
        copy = copy_to(*args)
        copy.start()
        sent.append(copy)
        return copy

    seq_dev = [((q + k) % 16, r) for k in range(16)]
    y_dev = [(((y + k) % 8) * 2 + zl, r) for k in range(8)]
    zl_dev = (y * 2 + 1 - zl, r)
    zh_dev = [(q, res(x, (zh + k) % 4, c)) for k in range(4)]
    x_dev = [(q, res((x + k) % 4, zh, c)) for k in range(4)]
    core_dev = (q, res(x, zh, 1 - c))
    relay_x, relay_zh = relay_of(plane, y, zl)
    relay_dev = (plane, res(relay_x, relay_zh, c))
    source = [[chunk_at(q, (x + 4 - i) % 4, (zh + 4 - j) % 4) for j in range(4)] for i in range(4)]
    held = [[source[i][j][0] * 2 + source[i][j][1] for j in range(4)] for i in range(4)]
    from_dev = (held[0][0], 2 * q + c)

    barrier = pltpu.get_barrier_semaphore()
    greet = seq_dev[1:] + zh_dev[1:] + x_dev[1:] + [core_dev, from_dev]
    for dev in greet:
        pl.semaphore_signal(barrier, inc=1, device_id=dev, device_id_type=MESH)

    loads = [
        pltpu.make_async_copy(a, b, load_sem.at[i])
        for i, (a, b) in enumerate(
            [(x_hbm, xv), (wc_hbm, wc), (wq_hbm, wq), (wk_hbm, wk), (wv_hbm, wv), (wg_hbm, wg),
             (wf_hbm, wf), (w1_hbm, w12t.at[0:32]), (w2_hbm, w12t.at[32:64]), (gain1_hbm, gain1),
             (shift1_hbm, shift1), (bg_hbm, bg), (bf_hbm, bf), (gain2_hbm, gain2),
             (shift2_hbm, shift2), (bc_hbm, bc)]
        )
    ]
    for copy in loads:
        copy.start()

    loads[0].wait()
    for i in range(16):
        for half in range(2):
            x32[half, i * 32:(i + 1) * 32, :] = xv[i, :, half * 128:(half + 1) * 128].astype(F32)
    for i in range(32):
        for half in range(2):
            xt[i, :, half * 128:(half + 1) * 128] = x32[half, pl.ds(i, 16, stride=32), :].astype(BF16)

    mine = pl.ds(pl.multiple_of(q * 16, 16), 16)
    for m in range(2):
        xg[m, mine, :] = xt[2 * q + m]

    pl.semaphore_wait(barrier, len(greet))
    order = (8, 7, 9, 6, 10, 5, 11, 4, 12, 3, 13, 2, 14, 1, 15)
    turn = [
        [go(seq_dev[k], xt.at[2 * seq_dev[k][0] + m], xg.at[m, mine, :], a_send, a_recv, m * 16 + k)
         for k in order]
        for m in range(2)
    ]

    for copy in loads[1:]:
        copy.wait()
    wt[0:256, :] = wq[...].astype(F32).T.astype(BF16)
    wt[256:512, :] = wv[...].astype(F32).T.astype(BF16)
    wt[512:768, :] = wg[...].astype(F32).T.astype(BF16)
    bg_t[...] = jnp.broadcast_to(bg[...], (128, 256)).T
    vtx[:, 32:48, :] = jnp.ones((HEADS, 16, 256), BF16)
    w32[...] = wc[...].astype(F32)

    @pl.loop(0, 32)
    def _(b):
        block = w32[pl.ds(b, 32, stride=32), :].astype(BF16)
        zero = jnp.zeros((32, 128), BF16)
        for i in range(4):
            rows = pl.ds(pl.multiple_of(b * 128 + i * 32, 32), 32)
            for j in range(4):
                bd[rows, j * 128:(j + 1) * 128] = block if i == j else zero

    def attend(m):
        given = xg[m].astype(F32)
        normed = norm_rows(given, gain1[...], shift1[...]).astype(BF16)
        keys = dot(normed, wk[...]).astype(BF16)
        qvg = dot_t(wt[...], normed)
        queries_t = qvg[0:256].astype(BF16)
        vtx[:, 0:32, :] = qvg[256:512].astype(BF16).reshape(HEADS, WIDTH, 256)
        gate_t = 1.0 / (1.0 + jnp.exp(-(qvg[512:768] + bg_t[:, 0:1])))
        for h in range(HEADS):
            group, place = h // 4, h % 4
            padded = jnp.concatenate(
                [
                    queries_t[h * WIDTH:(h + 1) * WIDTH, :] if i == place else jnp.zeros((WIDTH, 256), BF16)
                    for i in range(4)
                ],
                axis=0,
            )
            scores = dot(keys[:, group * 128:(group + 1) * 128], padded)
            top = jnp.max(scores, axis=0, keepdims=True)
            weights[h] = jnp.exp2((scores - top) * SCALE).astype(BF16)
        for h in range(HEADS):
            span = slice(h * WIDTH, (h + 1) * WIDTH)
            mixed = dot(vtx[h], weights[h])
            gated_t[span, :] = mixed[0:32] * (1.0 / mixed[32:33]) * gate_t[span, :]
        gated = gated_t[...].T.astype(BF16)
        attended = (dot(gated, wf[...]) + bf[...]).astype(BF16)
        updated = (given + attended.astype(F32)).astype(BF16)
        upd[m] = updated
        outer_normed = norm_rows(updated.astype(F32), gain2[...], shift2[...]).astype(BF16)
        both = dot_t(w12t[...], outer_normed).astype(BF16)
        lt[m] = both[0:32]
        rt[m] = both[32:64]

    def slot(c_, q_, m):
        return left.at[(c_ * 16 + q_) * 2 + m]

    relay, along, across, back = [], [], [], []
    for m in range(2):
        for copy in turn[m][::-1]:
            copy.wait_recv()
        attend(m)
        relay.append(go(relay_dev, lt.at[m], slot(c, q, m), p_send, p_recv, m))
        here = right.at[2 * q + m]
        across.append(go(zl_dev, rt.at[m], here, rz_send, rz_recv, m * 8))
        along.append(
            {k: go(y_dev[k], rt.at[m], here, ry_send, ry_recv, m * 8 + k) for k in SPREAD}
        )
        right[2 * q + m] = rt[m]
        upd_all[2 * q + m] = upd[m, mine, :]

    def send_back(m):
        for k in order:
            rows = pl.ds(pl.multiple_of(seq_dev[k][0] * 16, 16), 16)
            back.append(
                go(seq_dev[k], upd.at[m, rows, :], upd_all.at[2 * q + m], u_send, u_recv, m * 16 + k)
            )

    def pass_on(j, m):
        here = slot(c, held[0][j], m)
        for k in (2, 1, 3):
            go(x_dev[k], here, here, lx_send, lx_recv, m * 12 + j * 3 + k - 1)
        go(core_dev, here, here, lc_send, lc_recv, m * 16 + j)

    z_left = []
    for m in range(2):
        relay[m].wait_recv()
        here = slot(c, held[0][0], m)
        z_left.append({k: go(zh_dev[k], here, here, lz_send, lz_recv, m * 3 + k - 1) for k in (2, 1, 3)})
        pass_on(0, m)
        for k in SPREAD[::-1]:
            along[m][k].wait_recv()
            here = right.at[(((y + 8 - k) % 8) * 2 + zl) * 2 + m]
            across.append(go(zl_dev, here, here, rz_send, rz_recv, m * 8 + k))
    send_back(0)
    send_back(1)
    for m in range(2):
        for k in (1, 3, 2):
            z_left[m][k].wait_recv()
            pass_on(k, m)

    def outer_of(c_, m, pick):
        at = [(c_ * 16 + held[i][j]) * 2 + m for i, j in pick]
        rows = jnp.concatenate([left[n] for n in at], axis=0)
        for t in range(4):
            part = dot_t(right_p[t * 256:(t + 1) * 256, :], rows).astype(BF16)
            for b in range(8):
                lanes = slice(t * 1024 + b * 128, t * 1024 + (b + 1) * 128)
                for g in range(2):
                    outer[group_no[0] * 2 + g, :, lanes] = part[b * 32:(b + 1) * 32, g * 128:(g + 1) * 128]
        owner.extend(c_ * 16 + held[i][j] for i, j in pick)
        group_no[0] += 1

    group_no, owner = [0], []

    def pair_of(first, count, of):
        rows = outer[first:first + count].reshape(count * 32, 4096)
        total = dot(rows, bd[...]) * (1.0 / 256.0)
        for g in range(count):
            for i in range(4):
                pair[owner[(first + g) * 4 + i], of] = (
                    total[g * 32:(g + 1) * 32, i * 128:(i + 1) * 128] + bc[...]
                ).astype(BF16)

    FIRST = [(i, j) for j in (0, 1) for i in range(4)]
    SECOND = [(i, j) for j in (3, 2) for i in range(4)]

    def from_x(m):
        for j in (0, 1, 3, 2):
            for k in (1, 3, 2):
                here = slot(c, held[k][j], m)
                copy_to(x_dev[k], here, here, lx_send, lx_recv, m * 12 + j * 3 + k - 1).wait_recv()
                go(core_dev, here, here, lc_send, lc_recv, m * 16 + k * 4 + j)

    def from_core(m, pick):
        for k, j in pick:
            there = slot(1 - c, held[k][j], m)
            copy_to(core_dev, there, there, lc_send, lc_recv, m * 16 + k * 4 + j).wait_recv()

    from_x(0)
    for copy in across:
        copy.wait_recv()

    for i in range(32):
        for half in range(2):
            r32[half, i * 32:(i + 1) * 32, :] = right[i, :, half * 128:(half + 1) * 128].astype(F32)
    for b in range(32):
        for half in range(2):
            right_p[b * 32:(b + 1) * 32, half * 128:(half + 1) * 128] = r32[
                half, pl.ds(b, 32, stride=32), :
            ].astype(BF16)

    outer_of(c, 0, FIRST)
    outer_of(c, 0, SECOND)
    for pick in (FIRST, SECOND):
        from_core(0, pick)
        outer_of(1 - c, 0, pick)
    from_x(1)
    pair_of(0, 8, 0)
    outer_of(c, 1, FIRST)
    outer_of(c, 1, SECOND)
    for pick in (FIRST, SECOND):
        from_core(1, pick)
        outer_of(1 - c, 1, pick)
    pair_of(8, 8, 1)

    for copy in back:
        copy.wait_recv()
    for i in range(32):
        for half in range(2):
            x32[half, i * 16:(i + 1) * 16, :] = upd_all[i, :, half * 128:(half + 1) * 128].astype(F32)
    for i in range(16):
        for half in range(2):
            upd_v[i, :, half * 128:(half + 1) * 128] = x32[half, pl.ds(i, 32, stride=16), :].astype(BF16)
    for copy in sent:
        copy.wait_send()


def place(upd, pair, upd_out, pair_out, sems):
    copies = [
        pltpu.make_async_copy(pair, pair_out, sems.at[0]),
        pltpu.make_async_copy(upd, upd_out, sems.at[1]),
    ]
    for copy in copies:
        copy.start()
    for copy in copies:
        copy.wait()


def local(
    alignment_embedding, heed_layer_gain, heed_layer_shift, probe_weights, lookup_weights,
    content_weights, sigmoid_weights, sigmoid_shift, final_weights, final_shift,
    tensor_layer_gain, tensor_layer_shift, first_factor_weights, second_factor_weights,
    couple_weights, couple_shift,
):
    row = lambda a: a.reshape(1, -1)
    hbm = pl.BlockSpec(memory_space=pltpu.HBM)
    vmem = pl.BlockSpec(memory_space=pltpu.VMEM)
    at_hbm = lambda a: pltpu.with_memory_space_constraint(a, pltpu.HBM)
    at_vmem = lambda a: pltpu.with_memory_space_constraint(a, pltpu.VMEM)
    sem = pltpu.SemaphoreType.DMA
    buf = lambda *shape: pltpu.VMEM(shape, BF16)
    line = lambda n: pltpu.VMEM((1, n), F32)
    upd, pair = pl.pallas_call(
        kernel,
        out_shape=(
            pltpu.VMEM((16, 32, 256), BF16),
            pltpu.VMEM((32, 2, 32, 128), BF16),
        ),
        in_specs=[hbm] * 16,
        out_specs=(vmem, vmem),
        scratch_shapes=[
            buf(16, 32, 256), pltpu.VMEM((2, 512, 128), F32), buf(32, 16, 256), buf(2, 256, 256),
            line(256), line(256), line(256), line(256), line(256), line(256), line(128),
            buf(256, 256), buf(256, 256), buf(256, 256), buf(256, 256), buf(256, 256),
            buf(64, 256), buf(1024, 128), pltpu.VMEM((1024, 128), F32),
            buf(768, 256), pltpu.VMEM((256, 128), F32), buf(8, 48, 256), buf(8, 256, 256), pltpu.VMEM((256, 256), F32), buf(4096, 512),
            buf(2, 256, 256), buf(32, 16, 256), buf(2, 32, 256), buf(2, 32, 256),
            buf(64, 32, 256), buf(32, 32, 256), pltpu.VMEM((2, 1024, 128), F32), buf(1024, 256), buf(16, 32, 4096),
            sem((16,)), sem((32,)), sem((32,)), sem((32,)), sem((32,)), sem((2,)), sem((2,)),
            sem((16,)), sem((16,)), sem((16,)), sem((16,)), sem((6,)), sem((6,)),
            sem((24,)), sem((24,)), sem((32,)), sem((32,)),
        ],
        compiler_params=pltpu.CompilerParams(
            collective_id=0, has_side_effects=True, vmem_limit_bytes=44 * 2**20
        ),
        name="evoformer",
    )(
        *map(at_hbm, (
        alignment_embedding, row(heed_layer_gain), row(heed_layer_shift), probe_weights,
        lookup_weights, content_weights, sigmoid_weights, row(sigmoid_shift),
        final_weights, row(final_shift), row(tensor_layer_gain), row(tensor_layer_shift),
        first_factor_weights.T, second_factor_weights.T, couple_weights, row(couple_shift),
        ))
    )
    return pl.pallas_call(
        place,
        out_shape=(
            jax.ShapeDtypeStruct((16, 32, 256), BF16),
            jax.ShapeDtypeStruct((64, 32, 128), BF16),
        ),
        in_specs=[vmem, vmem],
        out_specs=(hbm, hbm),
        scratch_shapes=[sem((2,))],
        name="place",
    )(at_vmem(upd), at_vmem(pair.reshape(64, 32, 128)))


def solution(mesh):
    return jax.shard_map(
        local,
        mesh=mesh,
        in_specs=(P("seq", "res", None),) + (P(),) * 15,
        out_specs=(P("seq", "res", None), P("seq", "res", None)),
        check_vma=False,
    )
```

```python
import functools

import jax
import jax.numpy as jnp
from jax import lax
from jax.experimental import pallas as pl
from jax.experimental.pallas import tpu as pltpu
from jax.sharding import PartitionSpec as P

HEADS = 8
WIDTH = 32
BF16 = jnp.bfloat16
F32 = jnp.float32
MESH = pl.DeviceIdType.MESH
SPREAD = (4, 5, 3, 6, 2, 7, 1)
FARTHEST = (8, 7, 9, 6, 10, 5, 11, 4, 12, 3, 13, 2, 14, 1, 15)
SCALE = 1.4426950408889634 / 32.0**0.5


def norm_rows(values, scale, offset):
    center = values - jnp.mean(values, axis=-1, keepdims=True)
    spread = jnp.mean(center * center, axis=-1, keepdims=True)
    return center * lax.rsqrt(spread + 1e-05) * scale + offset


def dot(a, b):
    return jnp.dot(a, b, preferred_element_type=F32)


def dot_t(a, b):
    return lax.dot_general(a, b, (((1,), (1,)), ((), ())), preferred_element_type=F32)


def relay_of(p, y, zl):
    x, zh = p // 4, p % 4
    y_to, zl_to = p // 2, p % 2
    k = (y - y_to + 12) % 8
    dx = (2 * (k // 4) + 3 * (k % 2)) % 4
    far = ((k + 2) // 4) % 2
    e = (zl + zl_to) % 2
    s = 2 * zl_to - 1
    dz = (1 - e) * far * s + e * (far * 2 - (1 - far) * s)
    return (x + dx) % 4, (zh + dz + 8) % 4


def chunk_at(p, x, zh):
    x0, zh0 = p // 4, p % 4
    zl_to = p % 2
    s = 2 * zl_to - 1
    w = (x0 - x + 4) % 4
    u = ((zh - zh0 + 4) * (s + 4)) % 4
    e = u // 2
    far = ((u + 1) // 2) % 2
    k = w + (1 - far) * 4 * (w // 2) + 2 * far
    return (p // 2 + k + 4) % 8, (e + zl_to) % 2


def kernel(
    x_hbm, gain1_hbm, shift1_hbm, wq_hbm, wk_hbm, wv_hbm, wg_hbm, bg_hbm, wf_hbm, bf_hbm, gain2_hbm,
    shift2_hbm, w1_hbm, w2_hbm, wc_hbm, bc_hbm,
    upd_v, pair,
    xv, x32, xt, xg, gain1, shift1, bg, bf, gain2, shift2, bc, wq, wk, wv, wg, wf, w12t, wc, w32,
    wt, bg_t, vtx, weights, gated_t, bd,
    upd, upd_all, lt, rt, left, right, r32, right_p, outer,
    load_sem, a_send, a_recv, u_send, u_recv, p_send, p_recv, ry_send, ry_recv, rz_send, rz_recv,
    lz_send, lz_recv, lx_send, lx_recv, lc_send, lc_recv,
):
    q = lax.axis_index("seq")
    r = lax.axis_index("res")
    y, zl = q // 2, q % 2
    x, zh, c = r // 8, (r // 2) % 4, r % 2
    plane = r // 2

    def res(x_, zh_, c_):
        return (x_ * 4 + zh_) * 2 + c_

    sent = []

    def copy_to(dev, src, dst, ss, rs, i):
        return pltpu.make_async_remote_copy(
            src_ref=src, dst_ref=dst, send_sem=ss.at[i], recv_sem=rs.at[i], device_id=dev,
            device_id_type=MESH,
        )

    def go(*args):
        copy = copy_to(*args)
        copy.start()
        sent.append(copy)
        return copy

    seq_dev = [((q + k) % 16, r) for k in range(16)]
    y_dev = [(((y + k) % 8) * 2 + zl, r) for k in range(8)]
    zl_dev = (y * 2 + 1 - zl, r)
    barrier = pltpu.get_barrier_semaphore()
    for k in FARTHEST:
        pl.semaphore_signal(barrier, inc=1, device_id=seq_dev[k], device_id_type=MESH)
    zh_dev = [(q, res(x, (zh + k) % 4, c)) for k in range(4)]
    x_dev = [(q, res((x + k) % 4, zh, c)) for k in range(4)]
    core_dev = (q, res(x, zh, 1 - c))
    relay_x, relay_zh = relay_of(plane, y, zl)
    relay_dev = (plane, res(relay_x, relay_zh, c))
    from_y, from_zl = chunk_at(q, x, zh)
    others = zh_dev[1:] + x_dev[1:] + [core_dev, (from_y * 2 + from_zl, 2 * q + c)]
    for dev in others:
        pl.semaphore_signal(barrier, inc=1, device_id=dev, device_id_type=MESH)

    loads = [
        pltpu.make_async_copy(a, b, load_sem.at[i])
        for i, (a, b) in enumerate(
            [(x_hbm, xv), (wc_hbm, wc), (wq_hbm, wq), (wk_hbm, wk), (wv_hbm, wv), (wg_hbm, wg),
             (wf_hbm, wf), (w1_hbm, w12t.at[0:32]), (w2_hbm, w12t.at[32:64]), (gain1_hbm, gain1),
             (shift1_hbm, shift1), (bg_hbm, bg), (bf_hbm, bf), (gain2_hbm, gain2),
             (shift2_hbm, shift2), (bc_hbm, bc)]
        )
    ]
    for copy in loads:
        copy.start()

    loads[0].wait()
    for i in range(16):
        for half in range(2):
            x32[half, i * 32:(i + 1) * 32, :] = xv[i, :, half * 128:(half + 1) * 128].astype(F32)
    for i in range(32):
        for half in range(2):
            xt[i, :, half * 128:(half + 1) * 128] = x32[half, pl.ds(i, 16, stride=32), :].astype(BF16)

    mine = pl.ds(pl.multiple_of(q * 16, 16), 16)
    for m in range(2):
        xg[m, mine, :] = xt[2 * q + m]

    pl.semaphore_wait(barrier, 15 + len(others))
    order = FARTHEST
    turn = [
        [go(seq_dev[k], xt.at[2 * seq_dev[k][0] + m], xg.at[m, mine, :], a_send, a_recv, m * 16 + k)
         for k in order]
        for m in range(2)
    ]

    source = [[chunk_at(q, (x + 4 - i) % 4, (zh + 4 - j) % 4) for j in range(4)] for i in range(4)]
    held = [[source[i][j][0] * 2 + source[i][j][1] for j in range(4)] for i in range(4)]

    for copy in loads[1:]:
        copy.wait()
    wt[0:256, :] = wq[...].astype(F32).T.astype(BF16)
    wt[256:512, :] = wv[...].astype(F32).T.astype(BF16)
    wt[512:768, :] = wg[...].astype(F32).T.astype(BF16)
    bg_t[...] = jnp.broadcast_to(bg[...], (128, 256)).T
    vtx[:, 32:48, :] = jnp.ones((HEADS, 16, 256), BF16)
    w32[...] = wc[...].astype(F32)

    @pl.loop(0, 32)
    def _(b):
        block = w32[pl.ds(b, 32, stride=32), :].astype(BF16)
        zero = jnp.zeros((32, 128), BF16)
        for i in range(4):
            rows = pl.ds(pl.multiple_of(b * 128 + i * 32, 32), 32)
            for j in range(4):
                bd[rows, j * 128:(j + 1) * 128] = block if i == j else zero

    def attend(m):
        given = xg[m].astype(F32)
        normed = norm_rows(given, gain1[...], shift1[...]).astype(BF16)
        keys = dot(normed, wk[...]).astype(BF16)
        qvg = dot_t(wt[...], normed)
        queries_t = qvg[0:256].astype(BF16)
        vtx[:, 0:32, :] = qvg[256:512].astype(BF16).reshape(HEADS, WIDTH, 256)
        gate_t = 1.0 / (1.0 + jnp.exp(-(qvg[512:768] + bg_t[:, 0:1])))
        for h in range(HEADS):
            group, place = h // 4, h % 4
            padded = jnp.concatenate(
                [
                    queries_t[h * WIDTH:(h + 1) * WIDTH, :] if i == place else jnp.zeros((WIDTH, 256), BF16)
                    for i in range(4)
                ],
                axis=0,
            )
            scores = dot(keys[:, group * 128:(group + 1) * 128], padded)
            top = jnp.max(scores, axis=0, keepdims=True)
            weights[h] = jnp.exp2((scores - top) * SCALE).astype(BF16)
        for h in range(HEADS):
            span = slice(h * WIDTH, (h + 1) * WIDTH)
            mixed = dot(vtx[h], weights[h])
            gated_t[span, :] = mixed[0:32] * (1.0 / mixed[32:33]) * gate_t[span, :]
        gated = gated_t[...].T.astype(BF16)
        attended = (dot(gated, wf[...]) + bf[...]).astype(BF16)
        updated = (given + attended.astype(F32)).astype(BF16)
        upd[m] = updated
        outer_normed = norm_rows(updated.astype(F32), gain2[...], shift2[...]).astype(BF16)
        both = dot_t(w12t[...], outer_normed).astype(BF16)
        lt[m] = both[0:32]
        rt[m] = both[32:64]

    def slot(c_, q_, m):
        return left.at[(c_ * 16 + q_) * 2 + m]

    relay, along, across, back = [], [], [], []
    for m in range(2):
        for copy in turn[m][::-1]:
            copy.wait_recv()
        attend(m)
        relay.append(go(relay_dev, lt.at[m], slot(c, q, m), p_send, p_recv, m))
        here = right.at[2 * q + m]
        across.append(go(zl_dev, rt.at[m], here, rz_send, rz_recv, m * 8))
        along.append(
            {k: go(y_dev[k], rt.at[m], here, ry_send, ry_recv, m * 8 + k) for k in SPREAD}
        )
        right[2 * q + m] = rt[m]
        upd_all[2 * q + m] = upd[m, mine, :]

    def send_back(m):
        for k in order:
            rows = pl.ds(pl.multiple_of(seq_dev[k][0] * 16, 16), 16)
            back.append(
                go(seq_dev[k], upd.at[m, rows, :], upd_all.at[2 * q + m], u_send, u_recv, m * 16 + k)
            )

    def pass_on(j, m):
        here = slot(c, held[0][j], m)
        for k in (2, 1, 3):
            go(x_dev[k], here, here, lx_send, lx_recv, m * 12 + j * 3 + k - 1)
        go(core_dev, here, here, lc_send, lc_recv, m * 16 + j)

    z_left = []

    def take(m):
        relay[m].wait_recv()
        here = slot(c, held[0][0], m)
        z_left.append({k: go(zh_dev[k], here, here, lz_send, lz_recv, m * 3 + k - 1) for k in (2, 1, 3)})
        pass_on(0, m)

    def right_on(m):
        for k in SPREAD[::-1]:
            along[m][k].wait_recv()
            here = right.at[(((y + 8 - k) % 8) * 2 + zl) * 2 + m]
            across.append(go(zl_dev, here, here, rz_send, rz_recv, m * 8 + k))

    take(0)
    take(1)
    right_on(0)
    right_on(1)
    send_back(0)
    send_back(1)
    for m in range(2):
        for k in (1, 3, 2):
            z_left[m][k].wait_recv()
            pass_on(k, m)

    def outer_of(c_, m, pick):
        at = [(c_ * 16 + held[i][j]) * 2 + m for i, j in pick]
        rows = jnp.concatenate([left[n] for n in at], axis=0)
        for t in range(4):
            part = dot_t(right_p[t * 256:(t + 1) * 256, :], rows).astype(BF16)
            for b in range(8):
                lanes = slice(t * 1024 + b * 128, t * 1024 + (b + 1) * 128)
                for g in range(2):
                    outer[group_no[0] * 2 + g, :, lanes] = part[b * 32:(b + 1) * 32, g * 128:(g + 1) * 128]
        owner.extend(c_ * 16 + held[i][j] for i, j in pick)
        group_no[0] += 1

    group_no, owner = [0], []

    def pair_of(first, count, of):
        rows = outer[first:first + count].reshape(count * 32, 4096)
        total = dot(rows, bd[...]) * (1.0 / 256.0)
        for g in range(count):
            for i in range(4):
                pair[owner[(first + g) * 4 + i], of] = (
                    total[g * 32:(g + 1) * 32, i * 128:(i + 1) * 128] + bc[...]
                ).astype(BF16)

    FIRST = [(i, j) for j in (0, 1) for i in range(4)]
    SECOND = [(i, j) for j in (3, 2) for i in range(4)]

    def from_x(m):
        for j in (0, 1, 3, 2):
            for k in (1, 3, 2):
                here = slot(c, held[k][j], m)
                copy_to(x_dev[k], here, here, lx_send, lx_recv, m * 12 + j * 3 + k - 1).wait_recv()
                go(core_dev, here, here, lc_send, lc_recv, m * 16 + k * 4 + j)

    def from_core(m, pick):
        for k, j in pick:
            there = slot(1 - c, held[k][j], m)
            copy_to(core_dev, there, there, lc_send, lc_recv, m * 16 + k * 4 + j).wait_recv()

    from_x(0)
    for copy in across:
        copy.wait_recv()

    for i in range(32):
        for half in range(2):
            r32[half, i * 32:(i + 1) * 32, :] = right[i, :, half * 128:(half + 1) * 128].astype(F32)
    for b in range(32):
        for half in range(2):
            right_p[b * 32:(b + 1) * 32, half * 128:(half + 1) * 128] = r32[
                half, pl.ds(b, 32, stride=32), :
            ].astype(BF16)

    outer_of(c, 0, FIRST)
    outer_of(c, 0, SECOND)
    for pick in (FIRST, SECOND):
        from_core(0, pick)
        outer_of(1 - c, 0, pick)
    from_x(1)
    pair_of(0, 8, 0)
    outer_of(c, 1, FIRST)
    outer_of(c, 1, SECOND)
    for pick in (FIRST, SECOND):
        from_core(1, pick)
        outer_of(1 - c, 1, pick)
    pair_of(8, 8, 1)

    for copy in back:
        copy.wait_recv()
    for i in range(32):
        for half in range(2):
            x32[half, i * 16:(i + 1) * 16, :] = upd_all[i, :, half * 128:(half + 1) * 128].astype(F32)
    for i in range(16):
        for half in range(2):
            upd_v[i, :, half * 128:(half + 1) * 128] = x32[half, pl.ds(i, 32, stride=16), :].astype(BF16)
    for copy in sent:
        copy.wait_send()


def place(upd, pair, upd_out, pair_out, sems):
    copies = [
        pltpu.make_async_copy(pair, pair_out, sems.at[0]),
        pltpu.make_async_copy(upd, upd_out, sems.at[1]),
    ]
    for copy in copies:
        copy.start()
    for copy in copies:
        copy.wait()


def local(
    alignment_embedding, heed_layer_gain, heed_layer_shift, probe_weights, lookup_weights,
    content_weights, sigmoid_weights, sigmoid_shift, final_weights, final_shift,
    tensor_layer_gain, tensor_layer_shift, first_factor_weights, second_factor_weights,
    couple_weights, couple_shift,
):
    row = lambda a: a.reshape(1, -1)
    hbm = pl.BlockSpec(memory_space=pltpu.HBM)
    vmem = pl.BlockSpec(memory_space=pltpu.VMEM)
    at_hbm = lambda a: pltpu.with_memory_space_constraint(a, pltpu.HBM)
    at_vmem = lambda a: pltpu.with_memory_space_constraint(a, pltpu.VMEM)
    sem = pltpu.SemaphoreType.DMA
    buf = lambda *shape: pltpu.VMEM(shape, BF16)
    line = lambda n: pltpu.VMEM((1, n), F32)
    upd, pair = pl.pallas_call(
        kernel,
        out_shape=(
            pltpu.VMEM((16, 32, 256), BF16),
            pltpu.VMEM((32, 2, 32, 128), BF16),
        ),
        in_specs=[hbm] * 16,
        out_specs=(vmem, vmem),
        scratch_shapes=[
            buf(16, 32, 256), pltpu.VMEM((2, 512, 128), F32), buf(32, 16, 256), buf(2, 256, 256),
            line(256), line(256), line(256), line(256), line(256), line(256), line(128),
            buf(256, 256), buf(256, 256), buf(256, 256), buf(256, 256), buf(256, 256),
            buf(64, 256), buf(1024, 128), pltpu.VMEM((1024, 128), F32),
            buf(768, 256), pltpu.VMEM((256, 128), F32), buf(8, 48, 256), buf(8, 256, 256), pltpu.VMEM((256, 256), F32), buf(4096, 512),
            buf(2, 256, 256), buf(32, 16, 256), buf(2, 32, 256), buf(2, 32, 256),
            buf(64, 32, 256), buf(32, 32, 256), pltpu.VMEM((2, 1024, 128), F32), buf(1024, 256), buf(16, 32, 4096),
            sem((16,)), sem((32,)), sem((32,)), sem((32,)), sem((32,)), sem((2,)), sem((2,)),
            sem((16,)), sem((16,)), sem((16,)), sem((16,)), sem((6,)), sem((6,)),
            sem((24,)), sem((24,)), sem((32,)), sem((32,)),
        ],
        compiler_params=pltpu.CompilerParams(
            collective_id=0, has_side_effects=True, vmem_limit_bytes=44 * 2**20
        ),
        name="evoformer",
    )(
        *map(at_hbm, (
        alignment_embedding, row(heed_layer_gain), row(heed_layer_shift), probe_weights,
        lookup_weights, content_weights, sigmoid_weights, row(sigmoid_shift),
        final_weights, row(final_shift), row(tensor_layer_gain), row(tensor_layer_shift),
        first_factor_weights.T, second_factor_weights.T, couple_weights, row(couple_shift),
        ))
    )
    return pl.pallas_call(
        place,
        out_shape=(
            jax.ShapeDtypeStruct((16, 32, 256), BF16),
            jax.ShapeDtypeStruct((64, 32, 128), BF16),
        ),
        in_specs=[vmem, vmem],
        out_specs=(hbm, hbm),
        scratch_shapes=[sem((2,))],
        name="place",
    )(at_vmem(upd), at_vmem(pair.reshape(64, 32, 128)))


def solution(mesh):
    return jax.shard_map(
        local,
        mesh=mesh,
        in_specs=(P("seq", "res", None),) + (P(),) * 15,
        out_specs=(P("seq", "res", None), P("seq", "res", None)),
        check_vma=False,
    )
```

```python
import functools

import jax
import jax.numpy as jnp
from jax import lax
from jax.experimental import pallas as pl
from jax.experimental.pallas import tpu as pltpu
from jax.sharding import PartitionSpec as P

HEADS = 8
WIDTH = 32
BF16 = jnp.bfloat16
F32 = jnp.float32
MESH = pl.DeviceIdType.MESH
SPREAD = (4, 5, 3, 6, 2, 7, 1)
FARTHEST = (8, 7, 9, 6, 10, 5, 11, 4, 12, 3, 13, 2, 14, 1, 15)
SCALE = 1.4426950408889634 / 32.0**0.5


def norm_rows(values, scale, offset):
    center = values - jnp.mean(values, axis=-1, keepdims=True)
    spread = jnp.mean(center * center, axis=-1, keepdims=True)
    return center * lax.rsqrt(spread + 1e-05) * scale + offset


def dot(a, b):
    return jnp.dot(a, b, preferred_element_type=F32)


def dot_t(a, b):
    return lax.dot_general(a, b, (((1,), (1,)), ((), ())), preferred_element_type=F32)


def relay_of(p, y, zl):
    x, zh = p // 4, p % 4
    y_to, zl_to = p // 2, p % 2
    k = (y - y_to + 12) % 8
    dx = (2 * (k // 4) + 3 * (k % 2)) % 4
    far = ((k + 2) // 4) % 2
    e = (zl + zl_to) % 2
    s = 2 * zl_to - 1
    dz = (1 - e) * far * s + e * (far * 2 - (1 - far) * s)
    return (x + dx) % 4, (zh + dz + 8) % 4


def chunk_at(p, x, zh):
    x0, zh0 = p // 4, p % 4
    zl_to = p % 2
    s = 2 * zl_to - 1
    w = (x0 - x + 4) % 4
    u = ((zh - zh0 + 4) * (s + 4)) % 4
    e = u // 2
    far = ((u + 1) // 2) % 2
    k = w + (1 - far) * 4 * (w // 2) + 2 * far
    return (p // 2 + k + 4) % 8, (e + zl_to) % 2


def kernel(
    x_hbm, gain1_hbm, shift1_hbm, wq_hbm, wk_hbm, wv_hbm, wg_hbm, bg_hbm, wf_hbm, bf_hbm, gain2_hbm,
    shift2_hbm, w1_hbm, w2_hbm, wc_hbm, bc_hbm,
    upd_v, pair,
    xv, x32, xt, xg, gain1, shift1, bg, bf, gain2, shift2, bc, wq, wk, wv, wg, wf, w12t, wc, w32,
    wt, bg_t, vtx, weights, gated_t, bd,
    upd, upd_all, lt, rt, left, right, r32, right_p, outer,
    load_sem, a_send, a_recv, u_send, u_recv, p_send, p_recv, ry_send, ry_recv, rz_send, rz_recv,
    lz_send, lz_recv, lx_send, lx_recv, lc_send, lc_recv,
):
    q = lax.axis_index("seq")
    r = lax.axis_index("res")
    y, zl = q // 2, q % 2
    x, zh, c = r // 8, (r // 2) % 4, r % 2
    plane = r // 2

    def res(x_, zh_, c_):
        return (x_ * 4 + zh_) * 2 + c_

    sent = []

    def copy_to(dev, src, dst, ss, rs, i):
        return pltpu.make_async_remote_copy(
            src_ref=src, dst_ref=dst, send_sem=ss.at[i], recv_sem=rs.at[i], device_id=dev,
            device_id_type=MESH,
        )

    def go(*args):
        copy = copy_to(*args)
        copy.start()
        sent.append(copy)
        return copy

    seq_dev = [((q + k) % 16, r) for k in range(16)]
    y_dev = [(((y + k) % 8) * 2 + zl, r) for k in range(8)]
    zl_dev = (y * 2 + 1 - zl, r)
    barrier = pltpu.get_barrier_semaphore()
    for k in FARTHEST:
        pl.semaphore_signal(barrier, inc=1, device_id=seq_dev[k], device_id_type=MESH)
    zh_dev = [(q, res(x, (zh + k) % 4, c)) for k in range(4)]
    x_dev = [(q, res((x + k) % 4, zh, c)) for k in range(4)]
    core_dev = (q, res(x, zh, 1 - c))
    relay_x, relay_zh = relay_of(plane, y, zl)
    relay_dev = (plane, res(relay_x, relay_zh, c))
    from_y, from_zl = chunk_at(q, x, zh)
    others = zh_dev[1:] + x_dev[1:] + [core_dev, (from_y * 2 + from_zl, 2 * q + c)]
    for dev in others:
        pl.semaphore_signal(barrier, inc=1, device_id=dev, device_id_type=MESH)

    loads = [
        pltpu.make_async_copy(a, b, load_sem.at[i])
        for i, (a, b) in enumerate(
            [(x_hbm, xv), (wc_hbm, wc), (wq_hbm, wq), (wk_hbm, wk), (wv_hbm, wv), (wg_hbm, wg),
             (wf_hbm, wf), (w1_hbm, w12t.at[0:32]), (w2_hbm, w12t.at[32:64]), (gain1_hbm, gain1),
             (shift1_hbm, shift1), (bg_hbm, bg), (bf_hbm, bf), (gain2_hbm, gain2),
             (shift2_hbm, shift2), (bc_hbm, bc)]
        )
    ]
    for copy in loads:
        copy.start()

    loads[0].wait()
    for i in range(16):
        for half in range(2):
            x32[half, i * 32:(i + 1) * 32, :] = xv[i, :, half * 128:(half + 1) * 128].astype(F32)
    for i in range(32):
        for half in range(2):
            xt[i, :, half * 128:(half + 1) * 128] = x32[half, pl.ds(i, 16, stride=32), :].astype(BF16)

    mine = pl.ds(pl.multiple_of(q * 16, 16), 16)
    for m in range(2):
        xg[m, mine, :] = xt[2 * q + m]

    pl.semaphore_wait(barrier, 15 + len(others))
    order = FARTHEST
    turn = [
        [go(seq_dev[k], xt.at[2 * seq_dev[k][0] + m], xg.at[m, mine, :], a_send, a_recv, m * 16 + k)
         for k in order]
        for m in range(2)
    ]

    source = [[chunk_at(q, (x + 4 - i) % 4, (zh + 4 - j) % 4) for j in range(4)] for i in range(4)]
    held = [[source[i][j][0] * 2 + source[i][j][1] for j in range(4)] for i in range(4)]

    for copy in loads[1:]:
        copy.wait()
    wt[0:256, :] = wq[...].astype(F32).T.astype(BF16)
    wt[256:512, :] = wv[...].astype(F32).T.astype(BF16)
    wt[512:768, :] = wg[...].astype(F32).T.astype(BF16)
    bg_t[...] = jnp.broadcast_to(bg[...], (128, 256)).T
    vtx[:, 32:48, :] = jnp.ones((HEADS, 16, 256), BF16)
    w32[...] = wc[...].astype(F32)

    @pl.loop(0, 32)
    def _(b):
        block = w32[pl.ds(b, 32, stride=32), :].astype(BF16)
        zero = jnp.zeros((32, 128), BF16)
        for i in range(4):
            rows = pl.ds(pl.multiple_of(b * 128 + i * 32, 32), 32)
            for j in range(4):
                bd[rows, j * 128:(j + 1) * 128] = block if i == j else zero

    def attend(m):
        given = xg[m].astype(F32)
        normed = norm_rows(given, gain1[...], shift1[...]).astype(BF16)
        keys = dot(normed, wk[...]).astype(BF16)
        qvg = dot_t(wt[...], normed)
        queries_t = qvg[0:256].astype(BF16)
        vtx[:, 0:32, :] = qvg[256:512].astype(BF16).reshape(HEADS, WIDTH, 256)
        gate_t = 1.0 / (1.0 + jnp.exp(-(qvg[512:768] + bg_t[:, 0:1])))
        for h in range(HEADS):
            group, place = h // 4, h % 4
            padded = jnp.concatenate(
                [
                    queries_t[h * WIDTH:(h + 1) * WIDTH, :] if i == place else jnp.zeros((WIDTH, 256), BF16)
                    for i in range(4)
                ],
                axis=0,
            )
            scores = dot(keys[:, group * 128:(group + 1) * 128], padded)
            top = jnp.max(scores, axis=0, keepdims=True)
            weights[h] = jnp.exp2((scores - top) * SCALE).astype(BF16)
        for h in range(HEADS):
            span = slice(h * WIDTH, (h + 1) * WIDTH)
            mixed = dot(vtx[h], weights[h])
            gated_t[span, :] = mixed[0:32] * (1.0 / mixed[32:33]) * gate_t[span, :]
        gated = gated_t[...].T.astype(BF16)
        attended = (dot(gated, wf[...]) + bf[...]).astype(BF16)
        updated = (given + attended.astype(F32)).astype(BF16)
        upd[m] = updated
        outer_normed = norm_rows(updated.astype(F32), gain2[...], shift2[...]).astype(BF16)
        both = dot_t(w12t[...], outer_normed).astype(BF16)
        lt[m] = both[0:32]
        rt[m] = both[32:64]

    def slot(c_, q_, m):
        return left.at[(c_ * 16 + q_) * 2 + m]

    relay, along, across, back = [], [], [], []
    for m in range(2):
        for copy in turn[m][::-1]:
            copy.wait_recv()
        attend(m)
        relay.append(go(relay_dev, lt.at[m], slot(c, q, m), p_send, p_recv, m))
        here = right.at[2 * q + m]
        across.append(go(zl_dev, rt.at[m], here, rz_send, rz_recv, m * 8))
        along.append(
            {k: go(y_dev[k], rt.at[m], here, ry_send, ry_recv, m * 8 + k) for k in SPREAD}
        )
        right[2 * q + m] = rt[m]
        upd_all[2 * q + m] = upd[m, mine, :]

    def send_back(m):
        for k in order:
            rows = pl.ds(pl.multiple_of(seq_dev[k][0] * 16, 16), 16)
            back.append(
                go(seq_dev[k], upd.at[m, rows, :], upd_all.at[2 * q + m], u_send, u_recv, m * 16 + k)
            )

    def pass_on(j, m):
        here = slot(c, held[0][j], m)
        for k in (2, 1, 3):
            go(x_dev[k], here, here, lx_send, lx_recv, m * 12 + j * 3 + k - 1)
        go(core_dev, here, here, lc_send, lc_recv, m * 16 + j)

    z_left = []

    def take(m):
        relay[m].wait_recv()
        here = slot(c, held[0][0], m)
        z_left.append({k: go(zh_dev[k], here, here, lz_send, lz_recv, m * 3 + k - 1) for k in (2, 1, 3)})
        pass_on(0, m)

    def right_on(m):
        for k in SPREAD[::-1]:
            along[m][k].wait_recv()
            here = right.at[(((y + 8 - k) % 8) * 2 + zl) * 2 + m]
            across.append(go(zl_dev, here, here, rz_send, rz_recv, m * 8 + k))

    take(0)
    take(1)
    right_on(0)
    right_on(1)
    for m in range(2):
        for k in (1, 3, 2):
            z_left[m][k].wait_recv()
            pass_on(k, m)
    send_back(0)
    send_back(1)

    def outer_of(c_, m, pick):
        at = [(c_ * 16 + held[i][j]) * 2 + m for i, j in pick]
        rows = jnp.concatenate([left[n] for n in at], axis=0)
        for t in range(4):
            part = dot_t(right_p[t * 256:(t + 1) * 256, :], rows).astype(BF16)
            for b in range(8):
                lanes = slice(t * 1024 + b * 128, t * 1024 + (b + 1) * 128)
                for g in range(2):
                    outer[group_no[0] * 2 + g, :, lanes] = part[b * 32:(b + 1) * 32, g * 128:(g + 1) * 128]
        owner.extend(c_ * 16 + held[i][j] for i, j in pick)
        group_no[0] += 1

    group_no, owner = [0], []

    def pair_of(first, count, of):
        rows = outer[first:first + count].reshape(count * 32, 4096)
        total = dot(rows, bd[...]) * (1.0 / 256.0)
        for g in range(count):
            for i in range(4):
                pair[owner[(first + g) * 4 + i], of] = (
                    total[g * 32:(g + 1) * 32, i * 128:(i + 1) * 128] + bc[...]
                ).astype(BF16)

    FIRST = [(i, j) for j in (0, 1) for i in range(4)]
    SECOND = [(i, j) for j in (3, 2) for i in range(4)]

    def from_x(m):
        for j in (0, 1, 3, 2):
            for k in (1, 3, 2):
                here = slot(c, held[k][j], m)
                copy_to(x_dev[k], here, here, lx_send, lx_recv, m * 12 + j * 3 + k - 1).wait_recv()
                go(core_dev, here, here, lc_send, lc_recv, m * 16 + k * 4 + j)

    def from_core(m, pick):
        for k, j in pick:
            there = slot(1 - c, held[k][j], m)
            copy_to(core_dev, there, there, lc_send, lc_recv, m * 16 + k * 4 + j).wait_recv()

    from_x(0)
    for copy in across:
        copy.wait_recv()

    for i in range(32):
        for half in range(2):
            r32[half, i * 32:(i + 1) * 32, :] = right[i, :, half * 128:(half + 1) * 128].astype(F32)
    for b in range(32):
        for half in range(2):
            right_p[b * 32:(b + 1) * 32, half * 128:(half + 1) * 128] = r32[
                half, pl.ds(b, 32, stride=32), :
            ].astype(BF16)

    outer_of(c, 0, FIRST)
    outer_of(c, 0, SECOND)
    for pick in (FIRST, SECOND):
        from_core(0, pick)
        outer_of(1 - c, 0, pick)
    from_x(1)
    pair_of(0, 8, 0)
    outer_of(c, 1, FIRST)
    outer_of(c, 1, SECOND)
    for pick in (FIRST, SECOND):
        from_core(1, pick)
        outer_of(1 - c, 1, pick)
    pair_of(8, 8, 1)

    for copy in back:
        copy.wait_recv()
    for i in range(32):
        for half in range(2):
            x32[half, i * 16:(i + 1) * 16, :] = upd_all[i, :, half * 128:(half + 1) * 128].astype(F32)
    for i in range(16):
        for half in range(2):
            upd_v[i, :, half * 128:(half + 1) * 128] = x32[half, pl.ds(i, 32, stride=16), :].astype(BF16)
    for copy in sent:
        copy.wait_send()


def place(upd, pair, upd_out, pair_out, sems):
    copies = [
        pltpu.make_async_copy(pair, pair_out, sems.at[0]),
        pltpu.make_async_copy(upd, upd_out, sems.at[1]),
    ]
    for copy in copies:
        copy.start()
    for copy in copies:
        copy.wait()


def local(
    alignment_embedding, heed_layer_gain, heed_layer_shift, probe_weights, lookup_weights,
    content_weights, sigmoid_weights, sigmoid_shift, final_weights, final_shift,
    tensor_layer_gain, tensor_layer_shift, first_factor_weights, second_factor_weights,
    couple_weights, couple_shift,
):
    row = lambda a: a.reshape(1, -1)
    hbm = pl.BlockSpec(memory_space=pltpu.HBM)
    vmem = pl.BlockSpec(memory_space=pltpu.VMEM)
    at_hbm = lambda a: pltpu.with_memory_space_constraint(a, pltpu.HBM)
    at_vmem = lambda a: pltpu.with_memory_space_constraint(a, pltpu.VMEM)
    sem = pltpu.SemaphoreType.DMA
    buf = lambda *shape: pltpu.VMEM(shape, BF16)
    line = lambda n: pltpu.VMEM((1, n), F32)
    upd, pair = pl.pallas_call(
        kernel,
        out_shape=(
            pltpu.VMEM((16, 32, 256), BF16),
            pltpu.VMEM((32, 2, 32, 128), BF16),
        ),
        in_specs=[hbm] * 16,
        out_specs=(vmem, vmem),
        scratch_shapes=[
            buf(16, 32, 256), pltpu.VMEM((2, 512, 128), F32), buf(32, 16, 256), buf(2, 256, 256),
            line(256), line(256), line(256), line(256), line(256), line(256), line(128),
            buf(256, 256), buf(256, 256), buf(256, 256), buf(256, 256), buf(256, 256),
            buf(64, 256), buf(1024, 128), pltpu.VMEM((1024, 128), F32),
            buf(768, 256), pltpu.VMEM((256, 128), F32), buf(8, 48, 256), buf(8, 256, 256), pltpu.VMEM((256, 256), F32), buf(4096, 512),
            buf(2, 256, 256), buf(32, 16, 256), buf(2, 32, 256), buf(2, 32, 256),
            buf(64, 32, 256), buf(32, 32, 256), pltpu.VMEM((2, 1024, 128), F32), buf(1024, 256), buf(16, 32, 4096),
            sem((16,)), sem((32,)), sem((32,)), sem((32,)), sem((32,)), sem((2,)), sem((2,)),
            sem((16,)), sem((16,)), sem((16,)), sem((16,)), sem((6,)), sem((6,)),
            sem((24,)), sem((24,)), sem((32,)), sem((32,)),
        ],
        compiler_params=pltpu.CompilerParams(
            collective_id=0, has_side_effects=True, vmem_limit_bytes=44 * 2**20
        ),
        name="evoformer",
    )(
        *map(at_hbm, (
        alignment_embedding, row(heed_layer_gain), row(heed_layer_shift), probe_weights,
        lookup_weights, content_weights, sigmoid_weights, row(sigmoid_shift),
        final_weights, row(final_shift), row(tensor_layer_gain), row(tensor_layer_shift),
        first_factor_weights.T, second_factor_weights.T, couple_weights, row(couple_shift),
        ))
    )
    return pl.pallas_call(
        place,
        out_shape=(
            jax.ShapeDtypeStruct((16, 32, 256), BF16),
            jax.ShapeDtypeStruct((64, 32, 128), BF16),
        ),
        in_specs=[vmem, vmem],
        out_specs=(hbm, hbm),
        scratch_shapes=[sem((2,))],
        name="place",
    )(at_vmem(upd), at_vmem(pair.reshape(64, 32, 128)))


def solution(mesh):
    return jax.shard_map(
        local,
        mesh=mesh,
        in_specs=(P("seq", "res", None),) + (P(),) * 15,
        out_specs=(P("seq", "res", None), P("seq", "res", None)),
        check_vma=False,
    )
```
